32 devices in a mesh: group: 1, expert: 16 (over z, y, x), dp: 2 (over core).
Axes of the slice: x: 2, y: 2, z: 4, core: 2. Of those that a mesh axis runs over, the one named last changes fastest.
Arguments:
- tokens: bfloat16 [4, 256, 4096], P(None, ('group', 'expert', 'dp')), may hold values from -6 to 6
- routes: int32 [4, 256, 8], P(None, ('group', 'expert', 'dp')), may hold values from 0 to 15, all different within a row; in each aligned block of 8 rows (0 to 7, 8 to 15, ..., all dimensions but the last counted through in order) at most 4 rows name the same one
- route_weights: float32 [4, 256, 8], P(None, ('group', 'expert', 'dp')), may hold values from 0.05 to 1
- live_rows: int32 [4, 32], P(None, ('group', 'expert', 'dp')), may hold values from 4 to 8, as said below
- gate_weight: bfloat16 [16, 4096, 768], P('expert', None, 'dp'), may hold values from -0.09375 to 0.09375
- up_weight: bfloat16 [16, 4096, 768], P('expert', None, 'dp'), may hold values from -0.09375 to 0.09375
- down_weight: bfloat16 [16, 768, 4096], P('expert', 'dp'), may hold values from -0.21875 to 0.21875
Outputs:
- mixed: bfloat16 [4, 256, 4096], P(None, ('group', 'expert', 'dp'))
The draws below stay inside these ranges and needn't reach their ends.
Inputs may be any that keep to these rules, and one draw needn't show every extreme that they name: `routes`: in each step, of the 8 rows of one device at most 4 name any one expert, a bound that some block reaches of them; a row names 8 different experts. `live_rows`: in each step some device has all 8 rows live.
All inputs are finite; a program needn't handle non-finite values.
Results may differ from the reference program's by a relative error of at most 0.0059.
Values may be sent and summed in bfloat16 or wider, within the bound.
A program may use at most 128 MiB of HBM per device.

```python
import math
import jax
import jax.numpy as jnp
import numpy as np
from jax import lax

D = 4096
FF = 768
TOPK = 8
STEPS = 4
ROWS_DEV = 8
EXPERTS = 16
GROUP_DEVICES = 32
ROWS = 256
MOST = 4


def draw_live_rows(key, part):
    key = jax.random.fold_in(key, 7)
    first, second = jax.random.split(key)
    counts = jax.random.randint(first, (STEPS, GROUP_DEVICES), ROWS_DEV // 2, ROWS_DEV + 1)
    chosen = jax.random.randint(second, (STEPS, 1), 0, GROUP_DEVICES)
    column = jnp.arange(GROUP_DEVICES, dtype=jnp.int32)[None, :]
    return jnp.where(column == chosen, ROWS_DEV, counts).astype(jnp.int32)


def block_scale(rng, shape, shards, smallest, top_value):
    factor_of = 1.0
    for axis_at, blocks in shards:
        draws = jax.random.uniform(jax.random.fold_in(jax.random.fold_in(rng, 6), axis_at), (blocks,), jnp.float32, smallest / len(shards), top_value / len(shards))
        factor_of = factor_of * jnp.repeat(jnp.exp(draws), shape[axis_at] // blocks).reshape((-1,) + (1,) * (len(shape) - 1 - axis_at))
    return factor_of


def routed_block(own_key, own, number, rows, number_of, top, reach, skew):
    order = jax.random.permutation(own_key, number_of)
    heavy_load, ordinary = load_shares(number_of, rows * top, reach, skew, True), load_shares(number_of, rows * top, reach, skew, False)
    places = jnp.arange(number_of)

    def named(lengths, offset_by):
        used = int((lengths > 0).sum())
        fixed = max(1, used // 4)
        passed = fixed + (places - fixed + offset_by * (used - fixed)) % max(1, number_of - fixed)
        return jnp.zeros((number_of,), jnp.int32).at[order[jnp.where(places < fixed, places, passed)]].set(jnp.asarray(lengths, jnp.int32))

    lengths = jnp.where(number % 4 == 0, named(heavy_load, number // 4), named(ordinary, number - number // 4 - 1))
    mixed = jax.random.permutation(jax.random.fold_in(own, 3), number_of)
    giver, sink = mixed[0:number_of // 2 * 2:2], mixed[1:number_of // 2 * 2:2]
    room = jnp.minimum(lengths[giver] - 1, reach - lengths[sink]) // 2
    room = jnp.where((giver == order[0]) | (sink == order[0]) | (lengths[sink] == 0), 0, jnp.maximum(room, 0))
    passed = jax.random.randint(jax.random.fold_in(own, 4), (number_of // 2,), 0, 1 << 20) % (room + 1)
    lengths = lengths.at[giver].add(-passed).at[sink].add(passed)
    members = jnp.searchsorted(jnp.cumsum(lengths), jnp.arange(rows * top), side="right").astype(jnp.int32)
    table = members.reshape(top, rows).T
    table = table[jax.random.permutation(jax.random.fold_in(own, 1), rows)]
    offset_by = jax.random.randint(jax.random.fold_in(own, 2), (rows, 1), 0, top)
    return jnp.take_along_axis(table, (jnp.arange(top)[None, :] + offset_by) % top, axis=1)


def load_shares(number_of, total, most, lean, full):
    weights = [(1 << 20) // math.isqrt(standing ** lean) + 1 for standing in range(1, number_of + 1)]
    largest = most if full else min(most, max(-(-total // number_of), total * weights[0] // sum(weights)))
    least = 1 if total - largest >= number_of - 1 else 0
    given, spare = [largest] + [least] * (number_of - 1), total - largest - least * (number_of - 1)
    while spare > 0:
        free = [i for i in range(1, number_of) if given[i] < largest] or [i for i in range(1, number_of) if given[i] < most]
        mass, left = sum([weights[i] for i in free]), spare
        for i in free:
            extra = min(most - given[i], max(1, left * weights[i] // mass), spare)
            given[i] = given[i] + extra
            spare = spare - extra
    return np.array(given)


def bell_draw(rng, dims, spread, most, cuts=(), kind=jnp.bfloat16):
    values = jax.random.normal(rng, dims, jnp.float32) * spread
    if len(cuts) > 0:
        values = block_scale(rng, dims, cuts, -0.22, 0.18) * values
    return jnp.clip(values, min=-most, max=most).astype(kind)


def setup_inputs(seed: int = 0, part: int = 0) -> dict:
    streams_of = jax.random.split(jax.random.key(seed), 8)
    own_keys = jax.random.split(jax.random.fold_in(streams_of[7], part), 8)
    tokens = bell_draw(own_keys[0], (STEPS, ROWS, D), 1.0, 6.0, ((1, 32),))
    routes_keys = jax.random.split(jax.random.fold_in(own_keys[1], 1), STEPS * ROWS // ROWS_DEV)
    routes_turns = jax.random.permutation(jax.random.fold_in(own_keys[1], 3), STEPS * ROWS // ROWS_DEV)
    routes = jax.vmap(lambda own, number: routed_block(jax.random.fold_in(own_keys[1], 2), own, number, ROWS_DEV, EXPERTS, TOPK, MOST, 2))(routes_keys, routes_turns).reshape((STEPS, ROWS, TOPK))
    route_weights = jnp.clip(jnp.exp(math.log(1.0) - 2.9957323 * jax.random.uniform(own_keys[2], (STEPS, ROWS, TOPK), jnp.float32) ** block_scale(own_keys[2], (STEPS, ROWS, TOPK), ((1, 32),), -0.2, 0.2)), 0.05, 1.0)
    live_rows = draw_live_rows(jax.random.fold_in(jax.random.fold_in(streams_of[7], part), 71), part)
    gate_weight = bell_draw(streams_of[4], (EXPERTS, D, FF), D ** -0.5, 0.09375, ((0, 16), (2, 2)))
    up_weight = bell_draw(streams_of[5], (EXPERTS, D, FF), D ** -0.5, 0.09375, ((0, 16), (2, 2)))
    down_weight = bell_draw(streams_of[6], (EXPERTS, FF, D), FF ** -0.5, 0.21875, ((0, 16), (1, 2)))
    return {"tokens": tokens, "routes": routes, "route_weights": route_weights, "live_rows": live_rows, "gate_weight": gate_weight, "up_weight": up_weight, "down_weight": down_weight}


def one_step(rows_in, chosen, scores, counts, gate_weight, up_weight, down_weight):
    capacity = GROUP_DEVICES * MOST
    index = jnp.arange(ROWS, dtype=jnp.int32)
    live = (index % ROWS_DEV) < counts[index // ROWS_DEV]
    norm_weights = scores / jnp.sum(scores, axis=-1, keepdims=True)

    def per_expert(total, items):
        expert_id, gate_w, up_w, down_w = items
        hit = (chosen == expert_id) & live[:, None]
        member = jnp.any(hit, axis=1)
        weight_sum = jnp.sum(jnp.where(hit, norm_weights, 0.0), axis=1)
        position = jnp.cumsum(member.astype(jnp.int32)) - 1
        target = jnp.where(member, position, capacity).astype(jnp.int32)
        holder = jnp.zeros((capacity,), jnp.int32).at[target].set(index, mode="drop")
        filled = jnp.zeros((capacity,), jnp.float32).at[target].set(1.0, mode="drop")
        picked = rows_in[holder]
        gate = jnp.dot(picked, gate_w, preferred_element_type=jnp.float32)
        up = jnp.dot(picked, up_w, preferred_element_type=jnp.float32)
        hidden = (jax.nn.silu(gate) * up).astype(jnp.bfloat16)
        result = jnp.dot(hidden, down_w, preferred_element_type=jnp.float32).astype(jnp.bfloat16)
        result = lax.optimization_barrier(result).astype(jnp.float32)
        factor = weight_sum[holder] * filled
        return total.at[holder].add(factor[:, None] * result), None

    start = jnp.zeros((ROWS, D), jnp.float32)
    experts_ids = jnp.arange(EXPERTS, dtype=jnp.int32)
    total, _ = lax.scan(per_expert, start, (experts_ids, gate_weight, up_weight, down_weight))
    return total.astype(jnp.bfloat16)


def reference(tokens, routes, route_weights, live_rows, gate_weight, up_weight, down_weight):
    outputs = []
    for step in range(STEPS):
        outputs.append(one_step(tokens[step], routes[step], route_weights[step], live_rows[step],
                                gate_weight, up_weight, down_weight))
    return jnp.stack(outputs, axis=0)
```

```python
import jax
import jax.numpy as jnp
from jax import lax
from jax.sharding import PartitionSpec as P


def owner_scales(routes, route_weights, live_rows, experts_count):
    row_count = routes.shape[1]
    norm = route_weights / jnp.sum(route_weights, axis=-1, keepdims=True)
    alive = jnp.arange(row_count, dtype=jnp.int32)[None, :] < live_rows
    hit = routes[..., None] == jnp.arange(experts_count, dtype=jnp.int32)
    hit = hit & alive[:, :, None, None]
    return jnp.sum(jnp.where(hit, norm[..., None], 0.0), axis=2)


def shards(tokens, routes, route_weights, live_rows, gate_weight, up_weight, down_weight):
    steps, row_count, width = tokens.shape
    experts_count = lax.axis_size("expert")
    me = lax.axis_index("expert")
    gate_w, up_w, down_w = gate_weight[0], up_weight[0], down_weight[0]
    scales = owner_scales(routes, route_weights, live_rows, experts_count)
    all_scales = lax.all_gather(scales, ("expert", "dp"), axis=1, tiled=True)
    mine = jnp.sum(
        jnp.where(jnp.arange(experts_count) == me, all_scales, 0.0), axis=-1
    )
    rows = lax.all_gather(tokens, ("expert", "dp"), axis=1, tiled=True)
    rows_all = rows.shape[1]
    flat = rows.reshape(steps * rows_all, width)
    gate = jnp.dot(flat, gate_w, preferred_element_type=jnp.float32)
    up = jnp.dot(flat, up_w, preferred_element_type=jnp.float32)
    hidden = (jax.nn.silu(gate) * up).astype(jnp.bfloat16)
    part = jnp.dot(hidden, down_w, preferred_element_type=jnp.float32)
    part = part * mine.reshape(steps * rows_all, 1)
    part = part.reshape(steps, rows_all, width).astype(jnp.bfloat16)
    return lax.psum_scatter(part, ("expert", "dp"), scatter_dimension=1, tiled=True)


def solution(mesh):
    spread = ("group", "expert", "dp")
    in_specs = (
        P(None, spread, None),
        P(None, spread, None),
        P(None, spread, None),
        P(None, spread),
        P("expert", None, "dp"),
        P("expert", None, "dp"),
        P("expert", "dp", None),
    )
    out_specs = P(None, spread, None)
    return jax.shard_map(shards, mesh=mesh, in_specs=in_specs, out_specs=out_specs, check_vma=False)
```

```python
import functools

import jax
import jax.numpy as jnp
from jax import lax
from jax.experimental import pallas as pl
from jax.experimental.pallas import tpu as pltpu
from jax.sharding import PartitionSpec as P


def owner_scales(routes, route_weights, live_rows, experts_count):
    row_count = routes.shape[1]
    norm = route_weights / jnp.sum(route_weights, axis=-1, keepdims=True)
    alive = jnp.arange(row_count, dtype=jnp.int32)[None, :] < live_rows
    hit = routes[..., None] == jnp.arange(experts_count, dtype=jnp.int32)
    hit = hit & alive[:, :, None, None]
    return jnp.sum(jnp.where(hit, norm[..., None], 0.0), axis=2)

MESH = pl.DeviceIdType.MESH
CHUNKS = 8
TILE = 256
VMEM_BYTES = 56 * 2**20


def kernel(bits, chunks, tok, sc, gate_in, up_in, down_in, out,
           got, part, landed, scales, wgu, wd, acc, hidden, scale_col,
           ag_send, ag_recv, sc_send, sc_recv, rs_send, rs_recv,
           w_send, w_recv, w_local, t_local):
    me = lax.axis_index("expert")
    core = lax.axis_index("dp")
    other = {"dp": 1 - core}
    bit = [(me // 2**b) % 2 for b in range(bits)]
    partner = [{"expert": me + (1 - 2 * bit[b]) * 2**b} for b in range(bits)]
    rows, width = tok.shape
    cols = width // chunks
    half = gate_in.shape[1]
    full = 2 * half
    total = 2**bits * rows

    def gather_order(c):
        low = [0, 1] if c % 2 == 0 else [1, 0]
        return list(range(2, bits)) + low

    def reduce_order(c):
        return gather_order(c)[::-1]

    def place(free, flip=None):
        index = []
        for b in range(bits - 1, -1, -1):
            if b in free:
                index.append(slice(None))
            elif b == flip:
                index.append(1 - bit[b])
            else:
                index.append(bit[b])
        return tuple(index)

    barrier = pltpu.get_barrier_semaphore()
    for b in range(bits):
        pl.semaphore_signal(barrier, inc=1, device_id=partner[b], device_id_type=MESH)
    pl.semaphore_signal(barrier, inc=1, device_id=other, device_id_type=MESH)

    own = place(())
    locals_ = [pltpu.make_async_copy(tok.at[:, pl.ds(c * cols, cols)], got.at[(c, *own)], t_local.at[c])
               for c in range(chunks)]
    locals_.append(pltpu.make_async_copy(sc, scales.at[own], t_local.at[chunks]))
    for copy in locals_:
        copy.start()
    sources = [gate_in, up_in, down_in]

    def weight_slot(i, which):
        if i < 2:
            return wgu.at[:, pl.ds(i * full + which * half, half)]
        return wd.at[pl.ds(which * half, half), :]

    w_own = [pltpu.make_async_copy(sources[i], weight_slot(i, 0), w_local.at[i]) for i in range(3)]
    for copy in w_own:
        copy.start()
    pl.semaphore_wait(barrier, bits + 1)

    def ag_copy(c, level):
        order = gather_order(c)
        index = (c, *place(order[:level]))
        return pltpu.make_async_remote_copy(
            src_ref=got.at[index], dst_ref=got.at[index],
            send_sem=ag_send.at[c, level], recv_sem=ag_recv.at[c, level],
            device_id=partner[order[level]], device_id_type=MESH)

    def sc_copy(level):
        order = gather_order(0)
        index = place(order[:level])
        return pltpu.make_async_remote_copy(
            src_ref=scales.at[index], dst_ref=scales.at[index],
            send_sem=sc_send.at[level], recv_sem=sc_recv.at[level],
            device_id=partner[order[level]], device_id_type=MESH)

    def rs_copy(c, level):
        order = reduce_order(c)
        rest = order[level + 1:]
        b = order[level]
        return pltpu.make_async_remote_copy(
            src_ref=part.at[(c, *place(rest, b))], dst_ref=landed.at[(c, *place(rest))],
            send_sem=rs_send.at[c, level], recv_sem=rs_recv.at[c, level],
            device_id=partner[b], device_id_type=MESH)

    for c in range(chunks):
        locals_[c].wait()
        ag_copy(c, 0).start()
    locals_[chunks].wait()
    sc_copy(0).start()
    w_far = [pltpu.make_async_remote_copy(
        src_ref=sources[i], dst_ref=weight_slot(i, 1), send_sem=w_send.at[i],
        recv_sem=w_recv.at[i], device_id=other, device_id_type=MESH) for i in range(3)]
    for copy in w_far:
        copy.start()

    for level in range(bits):
        for c in range(chunks):
            ag_copy(c, level).wait_recv()
            if level + 1 < bits:
                ag_copy(c, level + 1).start()
                continue
            if c == 0:
                for i in range(2):
                    w_own[i].wait()
                    w_far[i].wait_recv()
            def up_tile(j, _, c=c):
                at = pl.ds(pl.multiple_of(j * TILE, TILE), TILE)
                x = got[c].reshape(total, cols)
                y = jnp.dot(x, wgu[pl.ds(c * cols, cols), at], preferred_element_type=jnp.float32)
                if c == 0:
                    acc[:, at] = y
                else:
                    acc[:, at] += y
                return 0

            lax.fori_loop(0, 2 * full // TILE, up_tile, 0)
        sc_copy(level).wait_recv()
        if level + 1 < bits:
            sc_copy(level + 1).start()

    def act_tile(j, _):
        at = pl.ds(pl.multiple_of(j * 128, 128), 128)
        gate = acc[:, at]
        up = acc[:, pl.ds(pl.multiple_of(full + j * 128, 128), 128)]
        hidden[:, at] = (gate / (1.0 + jnp.exp(-gate)) * up).astype(jnp.bfloat16)
        return 0

    lax.fori_loop(0, full // 128, act_tile, 0)
    every = scales[...].reshape(total, scales.shape[-1])
    lane = lax.broadcasted_iota(jnp.int32, every.shape, 1)
    column = jnp.sum(jnp.where(lane == me, every, 0.0), axis=1, keepdims=True)
    scale_col[...] = jnp.broadcast_to(column, scale_col.shape)
    w_own[2].wait()
    w_far[2].wait_recv()

    for c in range(chunks):
        def down_tile(j, _, c=c):
            at = pl.ds(pl.multiple_of(c * cols + j * TILE, TILE), TILE)
            y = jnp.dot(hidden[...], wd[:, at], preferred_element_type=jnp.float32)
            y = (y * scale_col[:, :1]).astype(jnp.bfloat16)
            to = (c, *([slice(None)] * (bits + 1)), pl.ds(pl.multiple_of(j * TILE, TILE), TILE))
            part[to] = y.reshape((2,) * bits + (rows, TILE))
            return 0

        lax.fori_loop(0, cols // TILE, down_tile, 0)
        rs_copy(c, 0).start()

    for level in range(bits):
        for c in range(chunks):
            rs_copy(c, level).wait_recv()
            order = reduce_order(c)
            rest, b = order[level + 1:], order[level]
            keep, came = (c, *place(rest)), (c, *place(rest, b))
            value = part[keep].astype(jnp.float32) + landed[came].astype(jnp.float32)
            if level + 1 < bits:
                part[keep] = value.astype(jnp.bfloat16)
                rs_copy(c, level + 1).start()
            else:
                out[:, pl.ds(c * cols, cols)] = value.astype(jnp.bfloat16)

    for level in range(bits):
        for c in range(chunks):
            ag_copy(c, level).wait_send()
            rs_copy(c, level).wait_send()
        sc_copy(level).wait_send()
    for copy in w_far:
        copy.wait_send()


def kernel_bytes(experts, rows, width, half):
    block = experts * rows
    return (3 * block * width * 2 + 3 * width * 2 * half * 2 + block * 4 * half * 4
            + block * 2 * half * 2 + 2 * block * 128 * 4 + 2 * rows * width * 2)


def fits(experts, rows, width, half, cores):
    even = experts >= 4 and experts & (experts - 1) == 0 and experts <= 128 and cores == 2
    return (even and rows % 16 == 0 and width % (CHUNKS * TILE) == 0 and half % 128 == 0
            and kernel_bytes(experts, rows, width, half) < VMEM_BYTES - 8 * 2**20)


def fused(tokens, routes, route_weights, live_rows, gate_weight, up_weight, down_weight):
    steps, row_count, width = tokens.shape
    experts = lax.axis_size("expert")
    bits = experts.bit_length() - 1
    rows = steps * row_count
    half = gate_weight.shape[2]
    scales = owner_scales(routes, route_weights, live_rows, experts)
    scales = jnp.pad(scales.reshape(rows, experts), ((0, 0), (0, 128 - experts)))
    cols = width // CHUNKS
    total = experts * rows
    grid = (2,) * bits
    dma = pltpu.SemaphoreType.DMA
    out = pl.pallas_call(
        functools.partial(kernel, bits, CHUNKS),
        out_shape=jax.ShapeDtypeStruct((rows, width), jnp.bfloat16),
        in_specs=[pl.BlockSpec(memory_space=pltpu.VMEM)] * 2
        + [pl.BlockSpec(memory_space=pl.ANY)] * 3,
        out_specs=pl.BlockSpec(memory_space=pltpu.VMEM),
        scratch_shapes=[
            pltpu.VMEM((CHUNKS, *grid, rows, cols), jnp.bfloat16),
            pltpu.VMEM((CHUNKS, *grid, rows, cols), jnp.bfloat16),
            pltpu.VMEM((CHUNKS, *grid, rows, cols), jnp.bfloat16),
            pltpu.VMEM((*grid, rows, 128), jnp.float32),
            pltpu.VMEM((width, 4 * half), jnp.bfloat16),
            pltpu.VMEM((2 * half, width), jnp.bfloat16),
            pltpu.VMEM((total, 4 * half), jnp.float32),
            pltpu.VMEM((total, 2 * half), jnp.bfloat16),
            pltpu.VMEM((total, 128), jnp.float32),
            dma((CHUNKS, bits)), dma((CHUNKS, bits)), dma((bits,)), dma((bits,)),
            dma((CHUNKS, bits)), dma((CHUNKS, bits)), dma((3,)), dma((3,)), dma((3,)),
            dma((CHUNKS + 1,)),
        ],
        compiler_params=pltpu.CompilerParams(
            collective_id=0, has_side_effects=True, vmem_limit_bytes=VMEM_BYTES),
        cost_estimate=pl.CostEstimate(
            flops=12 * total * half * width, bytes_accessed=12 * half * width, transcendentals=0),
    )(tokens.reshape(rows, width), scales, gate_weight[0], up_weight[0], down_weight[0])
    return out.reshape(steps, row_count, width)


def shards(tokens, routes, route_weights, live_rows, gate_weight, up_weight, down_weight):
    steps, row_count, width = tokens.shape
    experts_count = lax.axis_size("expert")
    if fits(experts_count, steps * row_count, width, gate_weight.shape[2], lax.axis_size("dp")):
        return fused(
            tokens, routes, route_weights, live_rows, gate_weight, up_weight, down_weight
        )
    me = lax.axis_index("expert")
    gate_w, up_w, down_w = gate_weight[0], up_weight[0], down_weight[0]
    scales = owner_scales(routes, route_weights, live_rows, experts_count)
    all_scales = lax.all_gather(scales, ("expert", "dp"), axis=1, tiled=True)
    mine = jnp.sum(
        jnp.where(jnp.arange(experts_count) == me, all_scales, 0.0), axis=-1
    )
    rows = lax.all_gather(tokens, ("expert", "dp"), axis=1, tiled=True)
    rows_all = rows.shape[1]
    flat = rows.reshape(steps * rows_all, width)
    gate = jnp.dot(flat, gate_w, preferred_element_type=jnp.float32)
    up = jnp.dot(flat, up_w, preferred_element_type=jnp.float32)
    hidden = (jax.nn.silu(gate) * up).astype(jnp.bfloat16)
    part = jnp.dot(hidden, down_w, preferred_element_type=jnp.float32)
    part = part * mine.reshape(steps * rows_all, 1)
    part = part.reshape(steps, rows_all, width).astype(jnp.bfloat16)
    return lax.psum_scatter(part, ("expert", "dp"), scatter_dimension=1, tiled=True)


def solution(mesh):
    spread = ("group", "expert", "dp")
    in_specs = (
        P(None, spread, None),
        P(None, spread, None),
        P(None, spread, None),
        P(None, spread),
        P("expert", None, "dp"),
        P("expert", None, "dp"),
        P("expert", "dp", None),
    )
    out_specs = P(None, spread, None)
    return jax.shard_map(shards, mesh=mesh, in_specs=in_specs, out_specs=out_specs, check_vma=False)
```

```python
import functools

import jax
import jax.numpy as jnp
from jax import lax
from jax.experimental import pallas as pl
from jax.experimental.pallas import tpu as pltpu
from jax.sharding import PartitionSpec as P


def owner_scales(routes, route_weights, live_rows, experts_count):
    row_count = routes.shape[1]
    norm = route_weights / jnp.sum(route_weights, axis=-1, keepdims=True)
    alive = jnp.arange(row_count, dtype=jnp.int32)[None, :] < live_rows
    hit = routes[..., None] == jnp.arange(experts_count, dtype=jnp.int32)
    hit = hit & alive[:, :, None, None]
    return jnp.sum(jnp.where(hit, norm[..., None], 0.0), axis=2)

MESH = pl.DeviceIdType.MESH
CHUNKS = 16
TILE = 256
ORDERS = ((1, 0, 1), (1, 1, 0), (0, 0, 1), (0, 1, 0))
LAG = 4
AHEAD = 16
VMEM_BYTES = 56 * 2**20


def kernel(bits, chunks, tok, sc, gate_in, up_in, down_in, out,
           got, part, landed, scales, wgu, wd, acc, hidden, scale_col,
           ag_send, ag_recv, sc_send, sc_recv, rs_send, rs_recv,
           w_send, w_recv, w_local, t_local):
    me = lax.axis_index("expert")
    core = lax.axis_index("dp")
    other = {"dp": 1 - core}
    bit = [(me // 2**b) % 2 for b in range(bits)]
    partner = [{"expert": me + (1 - 2 * bit[b]) * 2**b} for b in range(bits)]
    rows, width = tok.shape
    cols = width // chunks
    half = gate_in.shape[1]
    full = 2 * half
    total = 2**bits * rows

    def gather_order(c):
        high = list(range(bits - 1, 1, -1))
        choice = ORDERS[c % len(ORDERS)]
        first, second = choice[1:]
        if choice[0]:
            return [first] + high + [second]
        return high + [first, second]

    def reduce_order(c):
        return gather_order(c)[::-1]

    def place(free, flip=None):
        index = []
        for b in range(bits - 1, -1, -1):
            if b in free:
                index.append(slice(None))
            elif b == flip:
                index.append(1 - bit[b])
            else:
                index.append(bit[b])
        return tuple(index)

    barrier = pltpu.get_barrier_semaphore()
    for b in range(bits):
        pl.semaphore_signal(barrier, inc=1, device_id=partner[b], device_id_type=MESH)
    pl.semaphore_signal(barrier, inc=1, device_id=other, device_id_type=MESH)

    own = place(())
    locals_ = [pltpu.make_async_copy(tok.at[:, pl.ds(c * cols, cols)], got.at[(c, *own)], t_local.at[c])
               for c in range(chunks)]
    locals_.append(pltpu.make_async_copy(sc, scales.at[own], t_local.at[chunks]))
    for copy in locals_:
        copy.start()
    sources = [gate_in, up_in, down_in]

    def weight_slot(i, which):
        if i < 2:
            return wgu.at[:, pl.ds(i * full + which * half, half)]
        return wd.at[pl.ds(which * half, half), :]

    w_own = [pltpu.make_async_copy(sources[i], weight_slot(i, 0), w_local.at[i]) for i in range(3)]
    for copy in w_own:
        copy.start()
    pl.semaphore_wait(barrier, bits + 1)

    def ag_copy(c, level):
        order = gather_order(c)
        index = (c, *place(order[:level]))
        return pltpu.make_async_remote_copy(
            src_ref=got.at[index], dst_ref=got.at[index],
            send_sem=ag_send.at[c, level], recv_sem=ag_recv.at[c, level],
            device_id=partner[order[level]], device_id_type=MESH)

    def sc_copy(level):
        order = gather_order(0)
        index = place(order[:level])
        return pltpu.make_async_remote_copy(
            src_ref=scales.at[index], dst_ref=scales.at[index],
            send_sem=sc_send.at[level], recv_sem=sc_recv.at[level],
            device_id=partner[order[level]], device_id_type=MESH)

    def rs_copy(c, level):
        order = reduce_order(c)
        rest = order[level + 1:]
        b = order[level]
        return pltpu.make_async_remote_copy(
            src_ref=part.at[(c, *place(rest, b))], dst_ref=landed.at[(c, *place(rest))],
            send_sem=rs_send.at[c, level], recv_sem=rs_recv.at[c, level],
            device_id=partner[b], device_id_type=MESH)

    def wave(levels):
        pairs = [(c, level) for c in range(chunks) for level in range(levels)]
        return sorted(pairs, key=lambda p: (p[0] + LAG * p[1], -p[1]))

    def begin(c):
        locals_[c].wait()
        ag_copy(c, 0).start()

    for c in range(min(AHEAD, chunks)):
        begin(c)
    locals_[chunks].wait()
    sc_copy(0).start()
    w_far = [pltpu.make_async_remote_copy(
        src_ref=sources[i], dst_ref=weight_slot(i, 1), send_sem=w_send.at[i],
        recv_sem=w_recv.at[i], device_id=other, device_id_type=MESH) for i in range(3)]
    for copy in w_far:
        copy.start()

    for c, level in wave(bits):
        ag_copy(c, level).wait_recv()
        if level == 0 and c + AHEAD < chunks:
            begin(c + AHEAD)
        if level + 1 < bits:
            ag_copy(c, level + 1).start()
        else:
            if c == 0:
                for i in range(2):
                    w_own[i].wait()
                    w_far[i].wait_recv()

            def up_tile(j, _, c=c):
                at = pl.ds(pl.multiple_of(j * TILE, TILE), TILE)
                x = got[c].reshape(total, cols)
                y = jnp.dot(x, wgu[pl.ds(c * cols, cols), at], preferred_element_type=jnp.float32)
                if c == 0:
                    acc[:, at] = y
                else:
                    acc[:, at] += y
                return 0

            lax.fori_loop(0, 2 * full // TILE, up_tile, 0)
        if c == 0:
            sc_copy(level).wait_recv()
            if level + 1 < bits:
                sc_copy(level + 1).start()

    def act_tile(j, _):
        at = pl.ds(pl.multiple_of(j * 128, 128), 128)
        gate = acc[:, at]
        up = acc[:, pl.ds(pl.multiple_of(full + j * 128, 128), 128)]
        hidden[:, at] = (gate / (1.0 + jnp.exp(-gate)) * up).astype(jnp.bfloat16)
        return 0

    lax.fori_loop(0, full // 128, act_tile, 0)
    every = scales[...].reshape(total, scales.shape[-1])
    lane = lax.broadcasted_iota(jnp.int32, every.shape, 1)
    column = jnp.sum(jnp.where(lane == me, every, 0.0), axis=1, keepdims=True)
    scale_col[...] = jnp.broadcast_to(column, scale_col.shape)
    w_own[2].wait()
    w_far[2].wait_recv()

    for c, stage in wave(bits + 1):
        if stage == 0:
            def down_tile(j, _, c=c):
                at = pl.ds(pl.multiple_of(c * cols + j * TILE, TILE), TILE)
                y = jnp.dot(hidden[...], wd[:, at], preferred_element_type=jnp.float32)
                y = (y * scale_col[:, :1]).astype(jnp.bfloat16)
                to = (c, *([slice(None)] * (bits + 1)), pl.ds(pl.multiple_of(j * TILE, TILE), TILE))
                part[to] = y.reshape((2,) * bits + (rows, TILE))
                return 0

            lax.fori_loop(0, cols // TILE, down_tile, 0)
            rs_copy(c, 0).start()
            continue
        level = stage - 1
        rs_copy(c, level).wait_recv()
        order = reduce_order(c)
        rest, b = order[level + 1:], order[level]
        keep, came = (c, *place(rest)), (c, *place(rest, b))
        value = part[keep].astype(jnp.float32) + landed[came].astype(jnp.float32)
        if level + 1 < bits:
            part[keep] = value.astype(jnp.bfloat16)
            rs_copy(c, level + 1).start()
        else:
            out[:, pl.ds(c * cols, cols)] = value.astype(jnp.bfloat16)

    for level in range(bits):
        for c in range(chunks):
            ag_copy(c, level).wait_send()
            rs_copy(c, level).wait_send()
        sc_copy(level).wait_send()
    for copy in w_far:
        copy.wait_send()


def kernel_bytes(experts, rows, width, half):
    block = experts * rows
    return (3 * block * width * 2 + 3 * width * 2 * half * 2 + block * 4 * half * 4
            + block * 2 * half * 2 + 2 * block * 128 * 4 + 2 * rows * width * 2)


def fits(experts, rows, width, half, cores):
    even = experts >= 4 and experts & (experts - 1) == 0 and experts <= 128 and cores == 2
    return (even and rows % 16 == 0 and width % (CHUNKS * TILE) == 0 and half % 128 == 0
            and kernel_bytes(experts, rows, width, half) < VMEM_BYTES - 8 * 2**20)


def fused(tokens, routes, route_weights, live_rows, gate_weight, up_weight, down_weight):
    steps, row_count, width = tokens.shape
    experts = lax.axis_size("expert")
    bits = experts.bit_length() - 1
    rows = steps * row_count
    half = gate_weight.shape[2]
    scales = owner_scales(routes, route_weights, live_rows, experts)
    scales = jnp.pad(scales.reshape(rows, experts), ((0, 0), (0, 128 - experts)))
    cols = width // CHUNKS
    total = experts * rows
    grid = (2,) * bits
    dma = pltpu.SemaphoreType.DMA
    out = pl.pallas_call(
        functools.partial(kernel, bits, CHUNKS),
        out_shape=jax.ShapeDtypeStruct((rows, width), jnp.bfloat16),
        in_specs=[pl.BlockSpec(memory_space=pltpu.VMEM)] * 2
        + [pl.BlockSpec(memory_space=pl.ANY)] * 3,
        out_specs=pl.BlockSpec(memory_space=pltpu.VMEM),
        scratch_shapes=[
            pltpu.VMEM((CHUNKS, *grid, rows, cols), jnp.bfloat16),
            pltpu.VMEM((CHUNKS, *grid, rows, cols), jnp.bfloat16),
            pltpu.VMEM((CHUNKS, *grid, rows, cols), jnp.bfloat16),
            pltpu.VMEM((*grid, rows, 128), jnp.float32),
            pltpu.VMEM((width, 4 * half), jnp.bfloat16),
            pltpu.VMEM((2 * half, width), jnp.bfloat16),
            pltpu.VMEM((total, 4 * half), jnp.float32),
            pltpu.VMEM((total, 2 * half), jnp.bfloat16),
            pltpu.VMEM((total, 128), jnp.float32),
            dma((CHUNKS, bits)), dma((CHUNKS, bits)), dma((bits,)), dma((bits,)),
            dma((CHUNKS, bits)), dma((CHUNKS, bits)), dma((3,)), dma((3,)), dma((3,)),
            dma((CHUNKS + 1,)),
        ],
        compiler_params=pltpu.CompilerParams(
            collective_id=0, has_side_effects=True, vmem_limit_bytes=VMEM_BYTES),
        cost_estimate=pl.CostEstimate(
            flops=12 * total * half * width, bytes_accessed=12 * half * width, transcendentals=0),
    )(tokens.reshape(rows, width), scales, gate_weight[0], up_weight[0], down_weight[0])
    return out.reshape(steps, row_count, width)


def shards(tokens, routes, route_weights, live_rows, gate_weight, up_weight, down_weight):
    steps, row_count, width = tokens.shape
    experts_count = lax.axis_size("expert")
    if fits(experts_count, steps * row_count, width, gate_weight.shape[2], lax.axis_size("dp")):
        return fused(
            tokens, routes, route_weights, live_rows, gate_weight, up_weight, down_weight
        )
    me = lax.axis_index("expert")
    gate_w, up_w, down_w = gate_weight[0], up_weight[0], down_weight[0]
    scales = owner_scales(routes, route_weights, live_rows, experts_count)
    all_scales = lax.all_gather(scales, ("expert", "dp"), axis=1, tiled=True)
    mine = jnp.sum(
        jnp.where(jnp.arange(experts_count) == me, all_scales, 0.0), axis=-1
    )
    rows = lax.all_gather(tokens, ("expert", "dp"), axis=1, tiled=True)
    rows_all = rows.shape[1]
    flat = rows.reshape(steps * rows_all, width)
    gate = jnp.dot(flat, gate_w, preferred_element_type=jnp.float32)
    up = jnp.dot(flat, up_w, preferred_element_type=jnp.float32)
    hidden = (jax.nn.silu(gate) * up).astype(jnp.bfloat16)
    part = jnp.dot(hidden, down_w, preferred_element_type=jnp.float32)
    part = part * mine.reshape(steps * rows_all, 1)
    part = part.reshape(steps, rows_all, width).astype(jnp.bfloat16)
    return lax.psum_scatter(part, ("expert", "dp"), scatter_dimension=1, tiled=True)


def solution(mesh):
    spread = ("group", "expert", "dp")
    in_specs = (
        P(None, spread, None),
        P(None, spread, None),
        P(None, spread, None),
        P(None, spread),
        P("expert", None, "dp"),
        P("expert", None, "dp"),
        P("expert", "dp", None),
    )
    out_specs = P(None, spread, None)
    return jax.shard_map(shards, mesh=mesh, in_specs=in_specs, out_specs=out_specs, check_vma=False)
```

```python
import functools

import jax
import jax.numpy as jnp
from jax import lax
from jax.experimental import pallas as pl
from jax.experimental.pallas import tpu as pltpu
from jax.sharding import PartitionSpec as P


def owner_scales(routes, route_weights, live_rows, experts_count):
    row_count = routes.shape[1]
    norm = route_weights / jnp.sum(route_weights, axis=-1, keepdims=True)
    alive = jnp.arange(row_count, dtype=jnp.int32)[None, :] < live_rows
    hit = routes[..., None] == jnp.arange(experts_count, dtype=jnp.int32)
    hit = hit & alive[:, :, None, None]
    return jnp.sum(jnp.where(hit, norm[..., None], 0.0), axis=2)

MESH = pl.DeviceIdType.MESH
CHUNKS = 16
TILE = 256
ORDERS = ((1, 0, 1), (1, 1, 0), (0, 0, 1), (0, 1, 0))
GATHER_LAG = 4
REDUCE_LAG = 5
AHEAD = 6
VMEM_BYTES = 56 * 2**20


def kernel(bits, chunks, tok, sc, gate_in, up_in, down_in, out,
           got, part, landed, scales, wgu, wd, acc, hidden, scale_col,
           ag_send, ag_recv, sc_send, sc_recv, rs_send, rs_recv,
           w_send, w_recv, w_local, t_local):
    me = lax.axis_index("expert")
    core = lax.axis_index("dp")
    other = {"dp": 1 - core}
    bit = [(me // 2**b) % 2 for b in range(bits)]
    partner = [{"expert": me + (1 - 2 * bit[b]) * 2**b} for b in range(bits)]
    rows, width = tok.shape
    cols = width // chunks
    half = gate_in.shape[1]
    full = 2 * half
    total = 2**bits * rows

    def gather_order(c):
        high = list(range(bits - 1, 1, -1))
        choice = ORDERS[c % len(ORDERS)]
        first, second = choice[1:]
        if choice[0]:
            return [first] + high + [second]
        return high + [first, second]

    def reduce_order(c):
        return gather_order(c)[::-1]

    def place(free, flip=None):
        index = []
        for b in range(bits - 1, -1, -1):
            if b in free:
                index.append(slice(None))
            elif b == flip:
                index.append(1 - bit[b])
            else:
                index.append(bit[b])
        return tuple(index)

    barrier = pltpu.get_barrier_semaphore()
    for b in range(bits):
        pl.semaphore_signal(barrier, inc=1, device_id=partner[b], device_id_type=MESH)
    pl.semaphore_signal(barrier, inc=1, device_id=other, device_id_type=MESH)

    own = place(())
    locals_ = [pltpu.make_async_copy(tok.at[:, pl.ds(c * cols, cols)], got.at[(c, *own)], t_local.at[c])
               for c in range(chunks)]
    locals_.append(pltpu.make_async_copy(sc, scales.at[own], t_local.at[chunks]))
    for copy in locals_:
        copy.start()
    sources = [gate_in, up_in, down_in]

    def weight_slot(i, which):
        if i < 2:
            return wgu.at[:, pl.ds(i * full + which * half, half)]
        return wd.at[pl.ds(which * half, half), :]

    w_own = [pltpu.make_async_copy(sources[i], weight_slot(i, 0), w_local.at[i]) for i in range(3)]
    for copy in w_own:
        copy.start()
    pl.semaphore_wait(barrier, bits + 1)

    def ag_copy(c, level):
        order = gather_order(c)
        index = (c, *place(order[:level]))
        return pltpu.make_async_remote_copy(
            src_ref=got.at[index], dst_ref=got.at[index],
            send_sem=ag_send.at[c, level], recv_sem=ag_recv.at[c, level],
            device_id=partner[order[level]], device_id_type=MESH)

    def sc_copy(level):
        order = gather_order(0)
        index = place(order[:level])
        return pltpu.make_async_remote_copy(
            src_ref=scales.at[index], dst_ref=scales.at[index],
            send_sem=sc_send.at[level], recv_sem=sc_recv.at[level],
            device_id=partner[order[level]], device_id_type=MESH)

    def rs_copy(c, level):
        order = reduce_order(c)
        rest = order[level + 1:]
        b = order[level]
        return pltpu.make_async_remote_copy(
            src_ref=part.at[(c, *place(rest, b))], dst_ref=landed.at[(c, *place(rest))],
            send_sem=rs_send.at[c, level], recv_sem=rs_recv.at[c, level],
            device_id=partner[b], device_id_type=MESH)

    def wave(levels, lag):
        pairs = [(c, level) for c in range(chunks) for level in range(levels)]
        return sorted(pairs, key=lambda p: (p[0] + lag * p[1], -p[1]))

    def begin(c):
        locals_[c].wait()
        ag_copy(c, 0).start()

    for c in range(min(AHEAD, chunks)):
        begin(c)
    locals_[chunks].wait()
    sc_copy(0).start()
    w_far = [pltpu.make_async_remote_copy(
        src_ref=sources[i], dst_ref=weight_slot(i, 1), send_sem=w_send.at[i],
        recv_sem=w_recv.at[i], device_id=other, device_id_type=MESH) for i in range(3)]
    for copy in w_far:
        copy.start()

    for c, level in wave(bits, GATHER_LAG):
        ag_copy(c, level).wait_recv()
        if level == 0 and c + AHEAD < chunks:
            begin(c + AHEAD)
        if level + 1 < bits:
            ag_copy(c, level + 1).start()
        else:
            if c == 0:
                for i in range(2):
                    w_own[i].wait()
                    w_far[i].wait_recv()

            def up_tile(j, _, c=c):
                at = pl.ds(pl.multiple_of(j * TILE, TILE), TILE)
                x = got[c].reshape(total, cols)
                y = jnp.dot(x, wgu[pl.ds(c * cols, cols), at], preferred_element_type=jnp.float32)
                if c == 0:
                    acc[:, at] = y
                else:
                    acc[:, at] += y
                return 0

            lax.fori_loop(0, 2 * full // TILE, up_tile, 0)
        if c == 0:
            sc_copy(level).wait_recv()
            if level + 1 < bits:
                sc_copy(level + 1).start()

    def act_tile(j, _):
        at = pl.ds(pl.multiple_of(j * 128, 128), 128)
        gate = acc[:, at]
        up = acc[:, pl.ds(pl.multiple_of(full + j * 128, 128), 128)]
        hidden[:, at] = (gate / (1.0 + jnp.exp(-gate)) * up).astype(jnp.bfloat16)
        return 0

    lax.fori_loop(0, full // 128, act_tile, 0)
    every = scales[...].reshape(total, scales.shape[-1])
    lane = lax.broadcasted_iota(jnp.int32, every.shape, 1)
    column = jnp.sum(jnp.where(lane == me, every, 0.0), axis=1, keepdims=True)
    scale_col[...] = jnp.broadcast_to(column, scale_col.shape)
    w_own[2].wait()
    w_far[2].wait_recv()

    for c, stage in wave(bits + 1, REDUCE_LAG):
        if stage == 0:
            def down_tile(j, _, c=c):
                at = pl.ds(pl.multiple_of(c * cols + j * TILE, TILE), TILE)
                y = jnp.dot(hidden[...], wd[:, at], preferred_element_type=jnp.float32)
                y = (y * scale_col[:, :1]).astype(jnp.bfloat16)
                to = (c, *([slice(None)] * (bits + 1)), pl.ds(pl.multiple_of(j * TILE, TILE), TILE))
                part[to] = y.reshape((2,) * bits + (rows, TILE))
                return 0

            lax.fori_loop(0, cols // TILE, down_tile, 0)
            rs_copy(c, 0).start()
            continue
        level = stage - 1
        rs_copy(c, level).wait_recv()
        order = reduce_order(c)
        rest, b = order[level + 1:], order[level]
        keep, came = (c, *place(rest)), (c, *place(rest, b))
        value = part[keep].astype(jnp.float32) + landed[came].astype(jnp.float32)
        if level + 1 < bits:
            part[keep] = value.astype(jnp.bfloat16)
            rs_copy(c, level + 1).start()
        else:
            out[:, pl.ds(c * cols, cols)] = value.astype(jnp.bfloat16)

    for level in range(bits):
        for c in range(chunks):
            ag_copy(c, level).wait_send()
            rs_copy(c, level).wait_send()
        sc_copy(level).wait_send()
    for copy in w_far:
        copy.wait_send()


def kernel_bytes(experts, rows, width, half):
    block = experts * rows
    return (3 * block * width * 2 + 3 * width * 2 * half * 2 + block * 4 * half * 4
            + block * 2 * half * 2 + 2 * block * 128 * 4 + 2 * rows * width * 2)


def fits(experts, rows, width, half, cores):
    even = experts >= 4 and experts & (experts - 1) == 0 and experts <= 128 and cores == 2
    return (even and rows % 16 == 0 and width % (CHUNKS * TILE) == 0 and half % 128 == 0
            and kernel_bytes(experts, rows, width, half) < VMEM_BYTES - 8 * 2**20)


def fused(tokens, routes, route_weights, live_rows, gate_weight, up_weight, down_weight):
    steps, row_count, width = tokens.shape
    experts = lax.axis_size("expert")
    bits = experts.bit_length() - 1
    rows = steps * row_count
    half = gate_weight.shape[2]
    scales = owner_scales(routes, route_weights, live_rows, experts)
    scales = jnp.pad(scales.reshape(rows, experts), ((0, 0), (0, 128 - experts)))
    cols = width // CHUNKS
    total = experts * rows
    grid = (2,) * bits
    dma = pltpu.SemaphoreType.DMA
    out = pl.pallas_call(
        functools.partial(kernel, bits, CHUNKS),
        out_shape=jax.ShapeDtypeStruct((rows, width), jnp.bfloat16),
        in_specs=[pl.BlockSpec(memory_space=pltpu.VMEM)] * 2
        + [pl.BlockSpec(memory_space=pl.ANY)] * 3,
        out_specs=pl.BlockSpec(memory_space=pltpu.VMEM),
        scratch_shapes=[
            pltpu.VMEM((CHUNKS, *grid, rows, cols), jnp.bfloat16),
            pltpu.VMEM((CHUNKS, *grid, rows, cols), jnp.bfloat16),
            pltpu.VMEM((CHUNKS, *grid, rows, cols), jnp.bfloat16),
            pltpu.VMEM((*grid, rows, 128), jnp.float32),
            pltpu.VMEM((width, 4 * half), jnp.bfloat16),
            pltpu.VMEM((2 * half, width), jnp.bfloat16),
            pltpu.VMEM((total, 4 * half), jnp.float32),
            pltpu.VMEM((total, 2 * half), jnp.bfloat16),
            pltpu.VMEM((total, 128), jnp.float32),
            dma((CHUNKS, bits)), dma((CHUNKS, bits)), dma((bits,)), dma((bits,)),
            dma((CHUNKS, bits)), dma((CHUNKS, bits)), dma((3,)), dma((3,)), dma((3,)),
            dma((CHUNKS + 1,)),
        ],
        compiler_params=pltpu.CompilerParams(
            collective_id=0, has_side_effects=True, vmem_limit_bytes=VMEM_BYTES),
        cost_estimate=pl.CostEstimate(
            flops=12 * total * half * width, bytes_accessed=12 * half * width, transcendentals=0),
    )(tokens.reshape(rows, width), scales, gate_weight[0], up_weight[0], down_weight[0])
    return out.reshape(steps, row_count, width)


def shards(tokens, routes, route_weights, live_rows, gate_weight, up_weight, down_weight):
    steps, row_count, width = tokens.shape
    experts_count = lax.axis_size("expert")
    if fits(experts_count, steps * row_count, width, gate_weight.shape[2], lax.axis_size("dp")):
        return fused(
            tokens, routes, route_weights, live_rows, gate_weight, up_weight, down_weight
        )
    me = lax.axis_index("expert")
    gate_w, up_w, down_w = gate_weight[0], up_weight[0], down_weight[0]
    scales = owner_scales(routes, route_weights, live_rows, experts_count)
    all_scales = lax.all_gather(scales, ("expert", "dp"), axis=1, tiled=True)
    mine = jnp.sum(
        jnp.where(jnp.arange(experts_count) == me, all_scales, 0.0), axis=-1
    )
    rows = lax.all_gather(tokens, ("expert", "dp"), axis=1, tiled=True)
    rows_all = rows.shape[1]
    flat = rows.reshape(steps * rows_all, width)
    gate = jnp.dot(flat, gate_w, preferred_element_type=jnp.float32)
    up = jnp.dot(flat, up_w, preferred_element_type=jnp.float32)
    hidden = (jax.nn.silu(gate) * up).astype(jnp.bfloat16)
    part = jnp.dot(hidden, down_w, preferred_element_type=jnp.float32)
    part = part * mine.reshape(steps * rows_all, 1)
    part = part.reshape(steps, rows_all, width).astype(jnp.bfloat16)
    return lax.psum_scatter(part, ("expert", "dp"), scatter_dimension=1, tiled=True)


def solution(mesh):
    spread = ("group", "expert", "dp")
    in_specs = (
        P(None, spread, None),
        P(None, spread, None),
        P(None, spread, None),
        P(None, spread),
        P("expert", None, "dp"),
        P("expert", None, "dp"),
        P("expert", "dp", None),
    )
    out_specs = P(None, spread, None)
    return jax.shard_map(shards, mesh=mesh, in_specs=in_specs, out_specs=out_specs, check_vma=False)
```

```python
import functools

import jax
import jax.numpy as jnp
from jax import lax
from jax.experimental import pallas as pl
from jax.experimental.pallas import tpu as pltpu
from jax.sharding import PartitionSpec as P


def owner_scales(routes, route_weights, live_rows, experts_count):
    row_count = routes.shape[1]
    norm = route_weights / jnp.sum(route_weights, axis=-1, keepdims=True)
    alive = jnp.arange(row_count, dtype=jnp.int32)[None, :] < live_rows
    hit = routes[..., None] == jnp.arange(experts_count, dtype=jnp.int32)
    hit = hit & alive[:, :, None, None]
    return jnp.sum(jnp.where(hit, norm[..., None], 0.0), axis=2)

MESH = pl.DeviceIdType.MESH
CHUNKS = 16
TILE = 256
ORDERS = ((1, 0, 1), (1, 1, 0), (0, 0, 1), (0, 1, 0))
GATHER_LAG = 4
REDUCE_LAG = 5
AHEAD = 6
VMEM_BYTES = 56 * 2**20


def kernel(bits, chunks, tok, sc, gate_in, up_in, down_in, out,
           got, part, landed, scales, wgu, wd, acc, hidden, scale_col,
           ag_send, ag_recv, sc_send, sc_recv, rs_send, rs_recv,
           w_send, w_recv, w_local, t_local):
    me = lax.axis_index("expert")
    core = lax.axis_index("dp")
    other = {"dp": 1 - core}
    bit = [(me // 2**b) % 2 for b in range(bits)]
    partner = [{"expert": me + (1 - 2 * bit[b]) * 2**b} for b in range(bits)]
    rows, width = tok.shape
    cols = width // chunks
    half = gate_in.shape[1]
    full = 2 * half
    total = 2**bits * rows

    def gather_order(c):
        high = list(range(bits - 1, 1, -1))
        choice = ORDERS[c % len(ORDERS)]
        first, second = choice[1:]
        if choice[0]:
            return [first] + high + [second]
        return high + [first, second]

    def reduce_order(c):
        return gather_order(c)[::-1]

    def place(free, flip=None):
        index = []
        for b in range(bits - 1, -1, -1):
            if b in free:
                index.append(slice(None))
            elif b == flip:
                index.append(1 - bit[b])
            else:
                index.append(bit[b])
        return tuple(index)

    barrier = pltpu.get_barrier_semaphore()
    for b in range(bits):
        pl.semaphore_signal(barrier, inc=1, device_id=partner[b], device_id_type=MESH)
    pl.semaphore_signal(barrier, inc=1, device_id=other, device_id_type=MESH)

    own = place(())
    locals_ = [pltpu.make_async_copy(tok.at[:, pl.ds(c * cols, cols)], got.at[(c, *own)], t_local.at[c])
               for c in range(chunks)]
    locals_.append(pltpu.make_async_copy(sc, scales.at[own], t_local.at[chunks]))
    for copy in locals_:
        copy.start()
    sources = [gate_in, up_in, down_in]

    def weight_slot(i, which):
        if i < 2:
            return wgu.at[:, pl.ds(i * full + which * half, half)]
        return wd.at[pl.ds(which * half, half), :]

    w_own = [pltpu.make_async_copy(sources[i], weight_slot(i, 0), w_local.at[i]) for i in range(3)]
    for copy in w_own:
        copy.start()
    pl.semaphore_wait(barrier, bits + 1)

    def ag_copy(c, level):
        order = gather_order(c)
        index = (c, *place(order[:level]))
        return pltpu.make_async_remote_copy(
            src_ref=got.at[index] if level else tok.at[:, pl.ds(c * cols, cols)],
            dst_ref=got.at[index],
            send_sem=ag_send.at[c, level], recv_sem=ag_recv.at[c, level],
            device_id=partner[order[level]], device_id_type=MESH)

    def sc_copy(level):
        order = gather_order(0)
        index = place(order[:level])
        return pltpu.make_async_remote_copy(
            src_ref=scales.at[index], dst_ref=scales.at[index],
            send_sem=sc_send.at[level], recv_sem=sc_recv.at[level],
            device_id=partner[order[level]], device_id_type=MESH)

    def rs_copy(c, level):
        order = reduce_order(c)
        rest = order[level + 1:]
        b = order[level]
        return pltpu.make_async_remote_copy(
            src_ref=part.at[(c, *place(rest, b))], dst_ref=landed.at[(c, *place(rest))],
            send_sem=rs_send.at[c, level], recv_sem=rs_recv.at[c, level],
            device_id=partner[b], device_id_type=MESH)

    def wave(levels, lag):
        pairs = [(c, level) for c in range(chunks) for level in range(levels)]
        return sorted(pairs, key=lambda p: (p[0] + lag * p[1], -p[1]))

    def begin(c):
        ag_copy(c, 0).start()

    for c in range(min(AHEAD, chunks)):
        begin(c)
    locals_[chunks].wait()
    sc_copy(0).start()
    w_far = [pltpu.make_async_remote_copy(
        src_ref=sources[i], dst_ref=weight_slot(i, 1), send_sem=w_send.at[i],
        recv_sem=w_recv.at[i], device_id=other, device_id_type=MESH) for i in range(3)]
    for copy in w_far:
        copy.start()

    for c, level in wave(bits, GATHER_LAG):
        ag_copy(c, level).wait_recv()
        if level == 0:
            locals_[c].wait()
        if level == 0 and c + AHEAD < chunks:
            begin(c + AHEAD)
        if level + 1 < bits:
            ag_copy(c, level + 1).start()
        else:
            if c == 0:
                for i in range(2):
                    w_own[i].wait()
                    w_far[i].wait_recv()

            def up_tile(j, _, c=c):
                at = pl.ds(pl.multiple_of(j * TILE, TILE), TILE)
                x = got[c].reshape(total, cols)
                y = jnp.dot(x, wgu[pl.ds(c * cols, cols), at], preferred_element_type=jnp.float32)
                if c == 0:
                    acc[:, at] = y
                else:
                    acc[:, at] += y
                return 0

            lax.fori_loop(0, 2 * full // TILE, up_tile, 0)
        if c == 0:
            sc_copy(level).wait_recv()
            if level + 1 < bits:
                sc_copy(level + 1).start()

    def act_tile(j, _):
        at = pl.ds(pl.multiple_of(j * 128, 128), 128)
        gate = acc[:, at]
        up = acc[:, pl.ds(pl.multiple_of(full + j * 128, 128), 128)]
        hidden[:, at] = (gate / (1.0 + jnp.exp(-gate)) * up).astype(jnp.bfloat16)
        return 0

    lax.fori_loop(0, full // 128, act_tile, 0)
    every = scales[...].reshape(total, scales.shape[-1])
    lane = lax.broadcasted_iota(jnp.int32, every.shape, 1)
    column = jnp.sum(jnp.where(lane == me, every, 0.0), axis=1, keepdims=True)
    scale_col[...] = jnp.broadcast_to(column, scale_col.shape)
    w_own[2].wait()
    w_far[2].wait_recv()

    for c, stage in wave(bits + 1, REDUCE_LAG):
        if stage == 0:
            def down_tile(j, _, c=c):
                at = pl.ds(pl.multiple_of(c * cols + j * TILE, TILE), TILE)
                y = jnp.dot(hidden[...], wd[:, at], preferred_element_type=jnp.float32)
                y = (y * scale_col[:, :1]).astype(jnp.bfloat16)
                to = (c, *([slice(None)] * (bits + 1)), pl.ds(pl.multiple_of(j * TILE, TILE), TILE))
                part[to] = y.reshape((2,) * bits + (rows, TILE))
                return 0

            lax.fori_loop(0, cols // TILE, down_tile, 0)
            rs_copy(c, 0).start()
            continue
        level = stage - 1
        rs_copy(c, level).wait_recv()
        order = reduce_order(c)
        rest, b = order[level + 1:], order[level]
        keep, came = (c, *place(rest)), (c, *place(rest, b))
        value = part[keep].astype(jnp.float32) + landed[came].astype(jnp.float32)
        if level + 1 < bits:
            part[keep] = value.astype(jnp.bfloat16)
            rs_copy(c, level + 1).start()
        else:
            out[:, pl.ds(c * cols, cols)] = value.astype(jnp.bfloat16)

    for level in range(bits):
        for c in range(chunks):
            ag_copy(c, level).wait_send()
            rs_copy(c, level).wait_send()
        sc_copy(level).wait_send()
    for copy in w_far:
        copy.wait_send()


def kernel_bytes(experts, rows, width, half):
    block = experts * rows
    return (3 * block * width * 2 + 3 * width * 2 * half * 2 + block * 4 * half * 4
            + block * 2 * half * 2 + 2 * block * 128 * 4 + 2 * rows * width * 2)


def fits(experts, rows, width, half, cores):
    even = experts >= 4 and experts & (experts - 1) == 0 and experts <= 128 and cores == 2
    return (even and rows % 16 == 0 and width % (CHUNKS * TILE) == 0 and half % 128 == 0
            and kernel_bytes(experts, rows, width, half) < VMEM_BYTES - 8 * 2**20)


def fused(tokens, routes, route_weights, live_rows, gate_weight, up_weight, down_weight):
    steps, row_count, width = tokens.shape
    experts = lax.axis_size("expert")
    bits = experts.bit_length() - 1
    rows = steps * row_count
    half = gate_weight.shape[2]
    scales = owner_scales(routes, route_weights, live_rows, experts)
    scales = jnp.pad(scales.reshape(rows, experts), ((0, 0), (0, 128 - experts)))
    cols = width // CHUNKS
    total = experts * rows
    grid = (2,) * bits
    dma = pltpu.SemaphoreType.DMA
    out = pl.pallas_call(
        functools.partial(kernel, bits, CHUNKS),
        out_shape=jax.ShapeDtypeStruct((rows, width), jnp.bfloat16),
        in_specs=[pl.BlockSpec(memory_space=pltpu.VMEM)] * 2
        + [pl.BlockSpec(memory_space=pl.ANY)] * 3,
        out_specs=pl.BlockSpec(memory_space=pltpu.VMEM),
        scratch_shapes=[
            pltpu.VMEM((CHUNKS, *grid, rows, cols), jnp.bfloat16),
            pltpu.VMEM((CHUNKS, *grid, rows, cols), jnp.bfloat16),
            pltpu.VMEM((CHUNKS, *grid, rows, cols), jnp.bfloat16),
            pltpu.VMEM((*grid, rows, 128), jnp.float32),
            pltpu.VMEM((width, 4 * half), jnp.bfloat16),
            pltpu.VMEM((2 * half, width), jnp.bfloat16),
            pltpu.VMEM((total, 4 * half), jnp.float32),
            pltpu.VMEM((total, 2 * half), jnp.bfloat16),
            pltpu.VMEM((total, 128), jnp.float32),
            dma((CHUNKS, bits)), dma((CHUNKS, bits)), dma((bits,)), dma((bits,)),
            dma((CHUNKS, bits)), dma((CHUNKS, bits)), dma((3,)), dma((3,)), dma((3,)),
            dma((CHUNKS + 1,)),
        ],
        compiler_params=pltpu.CompilerParams(
            collective_id=0, has_side_effects=True, vmem_limit_bytes=VMEM_BYTES),
        cost_estimate=pl.CostEstimate(
            flops=12 * total * half * width, bytes_accessed=12 * half * width, transcendentals=0),
    )(tokens.reshape(rows, width), scales, gate_weight[0], up_weight[0], down_weight[0])
    return out.reshape(steps, row_count, width)


def shards(tokens, routes, route_weights, live_rows, gate_weight, up_weight, down_weight):
    steps, row_count, width = tokens.shape
    experts_count = lax.axis_size("expert")
    if fits(experts_count, steps * row_count, width, gate_weight.shape[2], lax.axis_size("dp")):
        return fused(
            tokens, routes, route_weights, live_rows, gate_weight, up_weight, down_weight
        )
    me = lax.axis_index("expert")
    gate_w, up_w, down_w = gate_weight[0], up_weight[0], down_weight[0]
    scales = owner_scales(routes, route_weights, live_rows, experts_count)
    all_scales = lax.all_gather(scales, ("expert", "dp"), axis=1, tiled=True)
    mine = jnp.sum(
        jnp.where(jnp.arange(experts_count) == me, all_scales, 0.0), axis=-1
    )
    rows = lax.all_gather(tokens, ("expert", "dp"), axis=1, tiled=True)
    rows_all = rows.shape[1]
    flat = rows.reshape(steps * rows_all, width)
    gate = jnp.dot(flat, gate_w, preferred_element_type=jnp.float32)
    up = jnp.dot(flat, up_w, preferred_element_type=jnp.float32)
    hidden = (jax.nn.silu(gate) * up).astype(jnp.bfloat16)
    part = jnp.dot(hidden, down_w, preferred_element_type=jnp.float32)
    part = part * mine.reshape(steps * rows_all, 1)
    part = part.reshape(steps, rows_all, width).astype(jnp.bfloat16)
    return lax.psum_scatter(part, ("expert", "dp"), scatter_dimension=1, tiled=True)


def solution(mesh):
    spread = ("group", "expert", "dp")
    in_specs = (
        P(None, spread, None),
        P(None, spread, None),
        P(None, spread, None),
        P(None, spread),
        P("expert", None, "dp"),
        P("expert", None, "dp"),
        P("expert", "dp", None),
    )
    out_specs = P(None, spread, None)
    return jax.shard_map(shards, mesh=mesh, in_specs=in_specs, out_specs=out_specs, check_vma=False)
```
